32 devices in a mesh: section: 4 (over y, x), tile: 8 (over z, core).
Axes of the slice: x: 2, y: 2, z: 4, core: 2. Of those that a mesh axis runs over, the one named last changes fastest.
Arguments:
- activations: bfloat16 [8, 8, 16, 16, 256], P('section', 'tile'), may hold values from -6 to 6
- weight: bfloat16 [4, 9, 256, 256], P('section'), may hold values from -0.125 to 0.125
- conv_bias: bfloat16 [4, 256], P('section'), may hold values from -3 to 3
- norm_gain: bfloat16 [4, 256], P('section'), may hold values from 0.099609375 to 1.8984375
- metric: bfloat16 [8, 9, 256], P('tile'), may hold values from 0.5 to 2
- neighbours: int32 [3, 8, 8], replicated, may hold values from 0 to 7, as said below
Outputs:
- advanced: bfloat16 [8, 8, 16, 16, 256], P('section', 'tile')
The draws below stay inside these ranges and needn't reach their ends.
Inputs may be any that keep to these rules, and one draw needn't show every extreme that they name: `neighbours`: row 0 names neighbour tiles; each of the 8 columns names every tile once. Row 1 is a side or corner number 0 to 3. Row 2 is 0 or 1 for the 4 side columns and 0 for the corner columns.
All inputs are finite; a program needn't handle non-finite values.
Results may differ from the reference program's by a relative error of at most 0.0075.
Values may be sent and summed in bfloat16 or wider, within the bound.
No kernel may reach another device: no remote copies, remote signals or barrier semaphores. Data moves between devices by JAX's collectives and lax.ppermute only.
A program may use at most 64 MiB of HBM per device.

```python
import math
import jax
import jax.numpy as jnp
from jax import lax

C = 256
SIDE = 16
TILES = 8
MICRO = 8
N_SECTION = 4


def draw_neighbours(key, part):
    key_tiles = jax.random.fold_in(key, 11)
    key_sides = jax.random.fold_in(key, 12)
    key_flips = jax.random.fold_in(key, 13)
    columns = [jax.random.permutation(jax.random.fold_in(key_tiles, column), TILES).astype(jnp.int32) for column in range(8)]
    tile_rows = jnp.stack(columns, axis=1)
    side_rows = jax.random.randint(key_sides, (TILES, 8), 0, 4).astype(jnp.int32)
    flip_sides = jax.random.randint(key_flips, (TILES, 4), 0, 2).astype(jnp.int32)
    flip_rows = jnp.concatenate([flip_sides, jnp.zeros((TILES, 4), jnp.int32)], axis=1)
    return jnp.stack([tile_rows, side_rows, flip_rows], axis=0)


def level_of(key, extent, cuts, least, top_value):
    def one(dim, shards_of):
        heights = jax.random.uniform(jax.random.fold_in(jax.random.fold_in(key, 6), dim), (shards_of,), jnp.float32, least / len(cuts), top_value / len(cuts))
        return jnp.repeat(jnp.exp(heights), extent[dim] // shards_of).reshape((-1,) + (1,) * (len(extent) - dim - 1))

    factor_of = one(*cuts[0])
    for cut in cuts[1:]:
        factor_of = factor_of * one(*cut)
    return factor_of


def noise(stream_key, dims, deviation, bound, cuts=(), kind=jnp.bfloat16):
    drawn = deviation * jax.random.normal(stream_key, dims, jnp.float32)
    if cuts:
        drawn = drawn * level_of(stream_key, dims, cuts, -0.22, 0.18)
    return jnp.clip(drawn, -bound, bound).astype(kind)


def setup_inputs(seed: int = 0) -> dict:
    key_of = jax.random.split(jax.random.key(seed), 7)
    return {
        "activations": noise(key_of[0], (MICRO, TILES, SIDE, SIDE, C), 1.0, 6.0, ((0, 4), (1, 8))),
        "weight": noise(key_of[1], (N_SECTION, 9, C, C), (9 * C) ** -0.5, 0.125, ((0, 4),)),
        "conv_bias": noise(key_of[2], (N_SECTION, C), 0.5, 3.0, ((0, 4),)),
        "norm_gain": jnp.clip(1.0 + 0.18 * jax.random.normal(key_of[3], (N_SECTION, C), jnp.float32), 0.099609375, 1.8984375).astype(jnp.bfloat16),
        "metric": jnp.clip(jnp.exp(math.log(2.0) - 1.3862944 * jax.random.uniform(key_of[4], (TILES, 9, SIDE * SIDE), jnp.float32) ** level_of(key_of[4], (TILES, 9, SIDE * SIDE), ((0, 8),), -0.2, 0.2)), 0.5, 2.0).astype(jnp.bfloat16),
        "neighbours": draw_neighbours(jax.random.fold_in(key_of[6], 71), 0),
    }


def normalize(states, gain_row):
    values = states.astype(jnp.float32)
    mean_sq = lax.optimization_barrier(jnp.mean(values * values, axis=-1, keepdims=True))
    return (values * lax.rsqrt(mean_sq + 1e-05) * gain_row.astype(jnp.float32)).astype(jnp.bfloat16)

def side_strips(normed):
    side_len = normed.shape[1]
    return jnp.stack([normed[:, 0], normed[:, :, side_len - 1], normed[:, side_len - 1], normed[:, :, 0]], axis=1)

def assemble(normed, strips, corners):
    top_row = jnp.concatenate([corners[0][:, None], strips[0], corners[1][:, None]], axis=1)
    middle = jnp.concatenate([strips[3][:, :, None], normed, strips[1][:, :, None]], axis=2)
    bottom = jnp.concatenate([corners[3][:, None], strips[2], corners[2][:, None]], axis=1)
    return jnp.concatenate([top_row[:, None], middle, bottom[:, None]], axis=1)

def convolve(padded, weight_taps, metric_taps, side_len):
    count = padded.shape[0]
    channels = padded.shape[-1]
    total = jnp.zeros((count, side_len * side_len, channels), jnp.float32)
    for row_off in range(3):
        for col_off in range(3):
            tap_index = row_off * 3 + col_off
            shifted = padded[:, row_off:row_off + side_len, col_off:col_off + side_len, :].reshape(-1, channels)
            product = jnp.dot(shifted, weight_taps[tap_index], preferred_element_type=jnp.float32)
            product = product.reshape(count, side_len * side_len, channels)
            total = total + product * metric_taps[:, tap_index, :, None].astype(jnp.float32)
    return total

def apply_layer(states, weight_taps, bias_row, gain_row, metric, neighbours):
    side_len = states.shape[1]
    channels = states.shape[-1]
    normed = normalize(states, gain_row)
    borders = side_strips(normed)
    strips = []
    for side_index in range(4):
        source = neighbours[0, :, side_index]
        which = neighbours[1, :, side_index]
        strip_rows = borders[source, which]
        strip_rows = jnp.where((neighbours[2, :, side_index] == 1)[:, None, None], strip_rows[:, ::-1], strip_rows)
        strips.append(strip_rows)
    corners = []
    for corner_index in range(4):
        source = neighbours[0, :, 4 + corner_index]
        which = neighbours[1, :, 4 + corner_index]
        rim_index = jnp.where(which < 2, 0, 2).astype(jnp.int32)
        position = jnp.where((which == 1) | (which == 2), side_len - 1, 0).astype(jnp.int32)
        corners.append(borders[source, rim_index, position])
    padded = assemble(normed, strips, corners)
    conv = convolve(padded, weight_taps, metric, side_len)
    conv = conv.reshape(states.shape)
    result = states.astype(jnp.float32) + jax.nn.silu(conv + bias_row.astype(jnp.float32))
    return result.astype(jnp.bfloat16)

def reference(activations, weight, conv_bias, norm_gain, metric, neighbours):
    sections = weight.shape[0]
    per_home = activations.shape[0] // sections
    homes = (jnp.arange(activations.shape[0]) // per_home).astype(jnp.int32)

    def one_micro(inputs):
        states, home_section = inputs
        for section_step in range(sections):
            layer_id = ((home_section + section_step) % sections).astype(jnp.int32)
            states = apply_layer(states, weight[layer_id], conv_bias[layer_id], norm_gain[layer_id], metric, neighbours)
        return states
    return lax.map(one_micro, (activations, homes))
```

```python
import functools

import jax
import jax.numpy as jnp
from jax import lax
from jax.experimental import pallas as pl
from jax.experimental.pallas import tpu as pltpu
from jax.sharding import PartitionSpec as P

BF16 = jnp.bfloat16
F32 = jnp.float32
EXTRA = 16


def swap(value, axis, by):
    peers = lax.axis_size(axis)
    return lax.ppermute(value, axis, [(i, i ^ by) for i in range(peers)])


def fetch(value, axis, by):
    peers = lax.axis_size(axis)
    return lax.ppermute(value, axis, [((i + by) % peers, i) for i in range(peers)])


def layer_kernel(side, tiles, outs, first, last, *refs):
    ids, near = refs[0], refs[1]
    refs = refs[2:]
    if first:
        even, odd, w, par, out = refs[:5]
        refs = refs[5:]
    else:
        even, odd, states, half_a, half_b, out = refs[:6]
        w, par, sem = refs[6:9]
        refs = refs[9:]
    center, pick, strips, pads, x = refs
    px = side * side
    ch = center.shape[-1]
    own = ids[0]
    core = ids[1]

    if not first:
        rows = half_a.shape[0] - EXTRA
        at_a = pl.multiple_of(core * rows, 128)
        at_b = pl.multiple_of((1 - core) * rows, 128)
        copies = [
            pltpu.make_async_copy(half_a.at[pl.ds(0, rows)], w.at[pl.ds(at_a, rows)], sem.at[0]),
            pltpu.make_async_copy(half_b.at[pl.ds(0, rows)], w.at[pl.ds(at_b, rows)], sem.at[1]),
            pltpu.make_async_copy(half_a.at[pl.ds(rows, EXTRA)], par, sem.at[2]),
        ]
        for copy in copies:
            copy.start()
        copies[2].wait()

    params = par[...].astype(F32)
    gain = params[0:1]
    bias = params[1:2]

    def load(j, odd_one):
        if first:
            return (odd if odd_one else even)[j, 0:px, :]
        return states[2 * j + odd_one]

    strip_rows = lax.broadcasted_iota(jnp.int32, (8 * side, px), 0)
    pixel = lax.broadcasted_iota(jnp.int32, (8 * side, px), 1)
    which = (strip_rows // side) % 4
    place = strip_rows % side
    place = jnp.where(strip_rows // side >= 4, side - 1 - place, place)
    wanted = jnp.where(
        which == 0,
        place,
        jnp.where(which == 1, place * side + side - 1, jnp.where(which == 2, px - side + place, place * side)),
    )
    pick[...] = jnp.where(pixel == wanted, 1.0, 0.0).astype(BF16)

    def prepare(j, odd_one):
        b = 2 * j + odd_one
        v = load(j, odd_one).astype(F32)
        mean_sq = jnp.mean(v * v, axis=-1, keepdims=True)
        z = (v * lax.rsqrt(mean_sq + 1e-05) * gain).astype(BF16)
        center[b] = z
        rims = jnp.dot(pick[...], z, preferred_element_type=F32)
        strips[b] = rims.reshape(8, side, ch)

    @pl.loop(0, tiles // 2)
    def _(j):
        prepare(j, 0)
        prepare(j, 1)

    if not first:
        copies[0].wait()
        copies[1].wait()

    col = lax.broadcasted_iota(jnp.int32, (side + 2, side, ch), 1)

    def build(b, j, odd_one, place):
        tile = own ^ b
        frame = []
        for s in range(4):
            frame.append(strips[own ^ near[0, tile, s], 4 * near[2, tile, s] + near[1, tile, s]])
        corner = []
        for k in range(4):
            which = near[1, tile, 4 + k]
            far = ((which == 1) | (which == 2)).astype(jnp.int32)
            rim_at = jnp.where(which < 2, 0, 2)
            corner.append(strips[own ^ near[0, tile, 4 + k], 4 * far + rim_at, 0:1])
        rows = center[b].astype(F32).reshape(side, side, ch)
        full = jnp.concatenate([frame[0][None], rows, frame[2][None]], axis=0)
        left = jnp.concatenate([corner[0], frame[3], corner[3]], axis=0)
        right = jnp.concatenate([corner[1], frame[1], corner[2]], axis=0)
        shape = (side + 2, side, ch)
        before = jnp.where(col == 0, jnp.broadcast_to(left[:, None, :], shape), pltpu.roll(full, 1, 1))
        after = jnp.where(col == side - 1, jnp.broadcast_to(right[:, None, :], shape), pltpu.roll(full, side - 1, 1))
        pads[0] = before.astype(BF16)
        pads[1] = full.astype(BF16)
        pads[2] = after.astype(BF16)
        metric = (odd if odd_one else even)[j, px : px + EXTRA, :].astype(F32)
        metric = jnp.transpose(metric)
        for q in range(9):
            a, c = q // 3, q % 3
            scale = jnp.broadcast_to(metric[:, q : q + 1], (px, ch)).astype(BF16)
            x[place * px : (place + 1) * px, q * ch : (q + 1) * ch] = pads[c, a : a + side].reshape(px, ch) * scale

    def finish(conv, j, odd_one, slot):
        u = conv + bias
        v = load(j, odd_one).astype(F32)
        out[slot] = (v + u / (1.0 + jnp.exp(-u))).astype(BF16)

    if last:
        build(0, 0, 0, 0)
        build(2, 1, 0, 1)
        conv = jnp.dot(x[...], w[...], preferred_element_type=F32)
        finish(conv[:px], 0, 0, 0)
        finish(conv[px:], 1, 0, 1)
    else:

        @pl.loop(0, tiles // 2)
        def _(j):
            build(2 * j, j, 0, 0)
            build(2 * j + 1, j, 1, 1)
            conv = jnp.dot(x[...], w[...], preferred_element_type=F32)
            finish(conv[:px], j, 0, 2 * j)
            finish(conv[px:], j, 1, 2 * j + 1)


def layer(first, last, ids, near, even, odd, states, weights):
    half = even.shape[0]
    tiles = 2 * half
    ch = even.shape[-1]
    px = even.shape[1] - EXTRA
    side = int(px**0.5)
    outs = 2 if last else tiles
    vmem = pl.BlockSpec(memory_space=pltpu.VMEM)
    smem = pl.BlockSpec(memory_space=pltpu.SMEM)
    hbm = pl.BlockSpec(memory_space=pl.ANY)
    scratch = [
        pltpu.VMEM((tiles, px, ch), BF16),
        pltpu.VMEM((8 * side, px), BF16),
        pltpu.VMEM((tiles, 8, side, ch), F32),
        pltpu.VMEM((3, side + 2, side, ch), BF16),
        pltpu.VMEM((2 * px, 9 * ch), BF16),
    ]
    if first:
        args = [ids, near, even, odd, *weights]
        specs = [smem, smem, vmem, vmem, vmem, vmem]
    else:
        args = [ids, near, even, odd, states, *weights]
        specs = [smem, smem, vmem, vmem, vmem, hbm, hbm]
        scratch = [pltpu.VMEM((9 * ch, ch), BF16), pltpu.VMEM((EXTRA, ch), BF16), pltpu.SemaphoreType.DMA((3,))] + scratch
    rows = outs * px
    return pl.pallas_call(
        functools.partial(layer_kernel, side, tiles, outs, first, last),
        out_shape=jax.ShapeDtypeStruct((outs, px, ch), BF16),
        in_specs=specs,
        out_specs=vmem,
        scratch_shapes=scratch,
        compiler_params=pltpu.CompilerParams(vmem_limit_bytes=48 * 2**20),
        cost_estimate=pl.CostEstimate(flops=2 * rows * 9 * ch * ch, bytes_accessed=4 * rows * ch, transcendentals=rows * ch),
    )(*args)


def local(activations, weight, conv_bias, norm_gain, metric, neighbours):
    sections = lax.axis_size("section")
    tiles = lax.axis_size("tile")
    own = lax.axis_index("tile")
    core = own & 1
    group = (own >> 1) & 1
    side, ch = activations.shape[2], activations.shape[-1]
    px = side * side
    ids = jnp.stack([own, core]).astype(jnp.int32)

    params = jnp.concatenate([norm_gain, conv_bias, jnp.zeros((EXTRA - 2, ch), BF16)], axis=0)
    flat = weight.reshape(-1, ch)
    rows = flat.shape[0] // 2
    half = jnp.concatenate([lax.dynamic_slice_in_dim(flat, core * rows, rows, 0), params], axis=0)
    halves = [fetch(half, "section", k) for k in range(1, sections)]

    extra = jnp.concatenate([metric[0].reshape(9, px), jnp.zeros((EXTRA - 9, px), BF16)], axis=0)
    batches = activations.reshape(2, px, ch)
    mine = jnp.concatenate([lax.dynamic_index_in_dim(batches, group, 0, False), extra], axis=0)
    other = jnp.concatenate([lax.dynamic_index_in_dim(batches, 1 - group, 0, False), extra], axis=0)
    even = [mine]
    for by in range(2, tiles, 2):
        even.append(swap(other if by & 2 else mine, "tile", by))
    even = jnp.stack(even)
    odd = swap(even, "tile", 1)

    states = layer(True, False, ids, neighbours, even, odd, None, (flat, params))
    for k in range(1, sections):
        a = halves[k - 1]
        states = layer(False, k == sections - 1, ids, neighbours, even, odd, states, (a, swap(a, "tile", 1)))
    kept = states[0]
    back = swap(states[1], "tile", 2)
    out = jnp.where(group == 0, jnp.stack([kept, back]), jnp.stack([back, kept]))
    return out.reshape(activations.shape)


def solution(mesh):
    in_specs = (
        P("section", "tile", None, None, None),
        P("section", None, None, None),
        P("section", None),
        P("section", None),
        P("tile", None, None),
        P(),
    )
    out_specs = P("section", "tile", None, None, None)
    return jax.shard_map(local, mesh=mesh, in_specs=in_specs, out_specs=out_specs, check_vma=False)
```

```python
import functools
import math

import jax
import jax.numpy as jnp
from jax import lax
from jax.experimental import pallas as pl
from jax.experimental.pallas import tpu as pltpu
from jax.sharding import PartitionSpec as P

BF16 = jnp.bfloat16
F32 = jnp.float32
EXTRA = 16
LANES = 128


def swap(value, axis, by):
    peers = lax.axis_size(axis)
    return lax.ppermute(value, axis, [(i, i ^ by) for i in range(peers)])


def fetch(value, axis, by):
    peers = lax.axis_size(axis)
    return lax.ppermute(value, axis, [((i + by) % peers, i) for i in range(peers)])


def ring_lines(side, depth):
    lines = []
    for d in range(depth):
        lines += [("row", d), ("row", side - 1 - d), ("col", d), ("col", side - 1 - d)]
    return lines


def weight_copies(core, half_a, half_b, w, par, sem):
    rows = half_a.shape[0] - EXTRA
    at_a = pl.multiple_of(core * rows, LANES)
    at_b = pl.multiple_of((1 - core) * rows, LANES)
    return [
        pltpu.make_async_copy(half_a.at[pl.ds(0, rows)], w.at[pl.ds(at_a, rows)], sem.at[0]),
        pltpu.make_async_copy(half_b.at[pl.ds(0, rows)], w.at[pl.ds(at_b, rows)], sem.at[1]),
        pltpu.make_async_copy(half_a.at[pl.ds(rows, EXTRA)], par, sem.at[2]),
    ]


def layer_kernel(side, tiles, source, depth_in, depth_out, started, *refs):
    refs = list(refs)
    take = lambda n: [refs.pop(0) for _ in range(n)]
    px = side * side
    ids, near = take(2)
    if source == "payload":
        even, odd = take(2)
    elif source == "full":
        even, odd, mt = take(3)
    else:
        kept_in, lines_in, mt = take(3)
    copied = source != "payload"
    weights = take(2)
    outs = take(2 if depth_out is None and source == "payload" or depth_out else 1)
    if copied:
        w, par, sem = take(3)
    else:
        w, par = weights
    zf, vtmp, vlines, fr, cr, pads, x, acc, xo, acco = take(10)
    if source == "payload":
        mt = outs[1]
    ch = x.shape[1] // 9
    halves = ch // LANES
    own, core = ids[0], ids[1]
    lines_out = ring_lines(side, depth_out or 0)
    step = min(64, px)
    chunks = [slice(i, i + step) for i in range(0, px, step)]

    if copied:
        copies = weight_copies(core, *weights, w, par, sem)
        if not started:
            for copy in copies:
                copy.start()
        copies[2].wait()
    gain = par[0:1, :].astype(F32)
    bias = par[1:2, :].astype(F32)

    def normed(part):
        mean_sq = jnp.mean(part * part, axis=-1, keepdims=True)
        return (part * lax.rsqrt(mean_sq + 1e-05) * gain).astype(BF16).astype(F32)

    def by_lanes(value):
        return [value[:, h * LANES : (h + 1) * LANES] for h in range(halves)]

    def at_line(kind, at):
        return pl.ds(at * side, side) if kind == "row" else pl.ds(at, side, stride=side)

    def normed_tile(b, read):
        for part in chunks:
            v = read(part)
            for h, value in enumerate(by_lanes(normed(v))):
                zf[b, h, part] = value
            if depth_out:
                for h, value in enumerate(by_lanes(v)):
                    vtmp[h, part] = value
        for n, (kind, at) in enumerate(lines_out):
            for h in range(halves):
                vlines[b, n, :, h * LANES : (h + 1) * LANES] = vtmp[h, at_line(kind, at), :].astype(BF16)

    def other(i):
        return jnp.where(i == 0, 1, i + 2)

    if source == "payload":

        @pl.loop(0, tiles // 2)
        def _(j):
            for ref, b in ((even, 2 * j), (odd, 2 * j + 1)):
                normed_tile(b, lambda part: ref[j, part].astype(F32))
                mt[b, :, 0:EXTRA] = jnp.transpose(ref[j, px : px + EXTRA, :].astype(F32))

    elif source == "full":

        @pl.loop(0, tiles // 2)
        def _(j):
            for ref, b in ((even, 2 * j), (odd, 2 * j + 1)):
                normed_tile(b, lambda part: ref[j, part].astype(F32))

    else:
        for place in range(2):
            for part in chunks:
                for h, value in enumerate(by_lanes(normed(kept_in[place, part].astype(F32)))):
                    zf[2 * place, h, part] = value
        lines = ring_lines(side, depth_in)

        @pl.loop(0, tiles - 2)
        def _(i):
            b = other(i)
            for first in range(0, len(lines), 4):
                z = normed(lines_in[i, first : first + 4].astype(F32).reshape(4 * side, ch))
                for n in range(4):
                    kind, at = lines[first + n]
                    for h, value in enumerate(by_lanes(z[n * side : (n + 1) * side])):
                        zf[b, h, at_line(kind, at), :] = value

    if copied:
        copies[0].wait()
        copies[1].wait()

    place_of = lax.broadcasted_iota(jnp.int32, (side, LANES), 0)
    eight = lax.broadcasted_iota(jnp.int32, (8, LANES), 0)
    first_place, last_place = place_of == 0, place_of == side - 1

    def frames(b):
        tile = own ^ b
        for s in range(4):
            src = own ^ near[0, tile, s]
            which = near[1, tile, s]
            flip = near[2, tile, s] == 1
            by_row = (which == 0) | (which == 2)
            at_row = pl.multiple_of(jnp.where(which == 0, 0, px - side), side)
            at_col = jnp.where(which == 1, side - 1, 0)
            for h in range(halves):
                line = jnp.where(by_row, zf[src, h, pl.ds(at_row, side), :], zf[src, h, pl.ds(at_col, side, stride=side), :])
                groups = [line[g : g + 8] for g in range(0, side, 8)]
                for n, group in enumerate(groups):
                    turned = pltpu.roll(groups[-1 - n], 4, 0)
                    for bit in (2, 1):
                        turned = jnp.where(eight & bit != 0, pltpu.roll(turned, bit, 0), pltpu.roll(turned, 8 - bit, 0))
                    fr[s, h, 8 * n : 8 * n + 8] = jnp.where(flip, turned, group)
        for k in range(4):
            src = own ^ near[0, tile, 4 + k]
            which = near[1, tile, 4 + k]
            at = jnp.where(which < 2, 0, px - side) + jnp.where((which == 1) | (which == 2), side - 1, 0)
            for h in range(halves):
                cr[k, h] = zf[src, h, pl.ds(at, 1), :]

    def spread(place, n, h, line, before, after):
        lanes = slice(h * LANES, (h + 1) * LANES)
        pads[place, n, 0, :, lanes] = jnp.where(first_place, before, pltpu.roll(line, 1, 0)).astype(BF16)
        pads[place, n, 1, :, lanes] = line.astype(BF16)
        pads[place, n, 2, :, lanes] = jnp.where(last_place, after, pltpu.roll(line, side - 1, 0)).astype(BF16)

    def spread_line(place, n, b, kind, at):
        low, high = (3, 1) if kind == "row" else (0, 2)
        for h in range(halves):
            if at < 0 or at >= side:
                edge = {("row", -1): (0, 0, 1), ("row", side): (2, 3, 2), ("col", -1): (3, 0, 3), ("col", side): (1, 1, 2)}
                s, k_before, k_after = edge[kind, at]
                spread(place, n, h, fr[s, h], cr[k_before, h], cr[k_after, h])
            else:
                line = zf[b, h, at_line(kind, at), :]
                spread(place, n, h, line, fr[low, h, at : at + 1], fr[high, h, at : at + 1])

    def build_tile(b, place):
        frames(b)
        for at in range(-1, side + 1):
            spread_line(place, at + 1, b, "row", at)
        metric = mt[b]
        for q in range(9):
            a, c = q // 3, q % 3
            taps = jnp.broadcast_to(metric[:, q : q + 1], (px, LANES)).astype(BF16)
            for lane in range(0, ch, LANES):
                x[place * px : (place + 1) * px, q * ch + lane : q * ch + lane + LANES] = (
                    pads[place, a : a + side, c, :, lane : lane + LANES].reshape(px, LANES) * taps
                )

    def build_lines(b, i):
        frames(b)
        slots = {}
        for kind, at in lines_out:
            for near_at in (at - 1, at, at + 1):
                if (kind, near_at) not in slots:
                    slots[kind, near_at] = len(slots)
                    spread_line(0, slots[kind, near_at], b, kind, near_at)
        for n, (kind, at) in enumerate(lines_out):
            metric = mt[b, at_line(kind, at), :]
            row = pl.multiple_of((i * len(lines_out) + n) * side, side)
            for q in range(9):
                a, c = q // 3, q % 3
                slot, seen = (slots[kind, at + a - 1], c) if kind == "row" else (slots[kind, at + c - 1], a)
                taps = jnp.broadcast_to(metric[:, q : q + 1], (side, LANES)).astype(BF16)
                for lane in range(0, ch, LANES):
                    lanes = slice(lane, lane + LANES)
                    xo[pl.ds(row, side), q * ch + lane : q * ch + lane + LANES] = pads[0, slot, seen, :, lanes] * taps

    def updated(v, conv):
        u = conv + bias
        return (v.astype(F32) + u / (1.0 + jnp.exp(-u))).astype(BF16)

    if depth_out is None:

        @pl.loop(0, tiles // 4)
        def _(j):
            build_tile(4 * j, 0)
            build_tile(4 * j + 2, 1)
            acc[...] = jnp.dot(x[...], w[...], preferred_element_type=F32)
            for place in range(2):
                for part in chunks:
                    conv = acc[place * px + part.start : place * px + part.stop]
                    outs[0][2 * j + place, part] = updated(even[2 * j + place, part], conv)

    else:
        build_tile(0, 0)
        build_tile(2, 1)
        acc[...] = jnp.dot(x[...], w[...], preferred_element_type=F32)
        for place in range(2):
            for part in chunks:
                v = even[place, part] if source == "full" else kept_in[place, part]
                outs[0][place, part] = updated(v, acc[place * px + part.start : place * px + part.stop])
        if depth_out:

            @pl.loop(0, tiles - 2)
            def _(i):
                build_lines(other(i), i)

            acco[...] = jnp.dot(xo[...], w[...], preferred_element_type=F32)

            @pl.loop(0, tiles - 2)
            def _(i):
                count = len(lines_out)
                for first in range(0, count, 4):
                    v = vlines[other(i), first : first + 4] if source == "full" else lines_in[i, first : first + 4]
                    at = pl.multiple_of((i * count + first) * side, side)
                    new = updated(v.reshape(4 * side, ch), acco[pl.ds(at, 4 * side)])
                    outs[1][i, first : first + 4] = new.reshape(4, side, ch)


def pack_kernel(ids, batches, metric, flat, gain, bias, mine, other, half, sem):
    px, ch = batches.shape[1:]
    rows = half.shape[0] - EXTRA
    start = pl.multiple_of(ids[1] * rows, LANES)
    copies = [
        pltpu.make_async_copy(batches.at[ids[2]], mine.at[pl.ds(0, px)], sem.at[0]),
        pltpu.make_async_copy(batches.at[1 - ids[2]], other.at[pl.ds(0, px)], sem.at[1]),
        pltpu.make_async_copy(flat.at[pl.ds(start, rows)], half.at[pl.ds(0, rows)], sem.at[2]),
    ]
    for copy in copies:
        copy.start()
    spare = jnp.concatenate([metric[...], jnp.zeros((EXTRA - 9, px), BF16)], axis=0)
    mine[px : px + EXTRA, :] = spare
    other[px : px + EXTRA, :] = spare
    half[rows : rows + EXTRA, :] = jnp.concatenate([gain[...], bias[...], jnp.zeros((EXTRA - 2, ch), BF16)], axis=0)
    for copy in copies:
        copy.wait()


def pack(ids, batches, metric, flat, gain, bias):
    state = jax.ShapeDtypeStruct((batches.shape[1] + EXTRA, batches.shape[2]), BF16)
    half = jax.ShapeDtypeStruct((flat.shape[0] // 2 + EXTRA, flat.shape[1]), BF16)
    return pl.pallas_call(
        pack_kernel,
        out_shape=(state, state, half),
        in_specs=[SMEM, HBM, VMEM, HBM, VMEM, VMEM],
        out_specs=(VMEM, VMEM, VMEM),
        scratch_shapes=[pltpu.SemaphoreType.DMA((3,))],
        compiler_params=pltpu.CompilerParams(vmem_limit_bytes=60 * 2**20),
    )(ids, batches, metric, flat, gain, bias)


VMEM = pl.BlockSpec(memory_space=pltpu.VMEM)
SMEM = pl.BlockSpec(memory_space=pltpu.SMEM)
HBM = pl.BlockSpec(memory_space=pl.ANY)


def last_layers_kernel(side, tiles, *refs):
    ids, near, even, odd, mt, a3, b3, a4, b4, out, kept, lines = refs[:12]
    w3, par3, sem3, w4, par4, sem4 = refs[12:18]
    space = refs[18:]
    for copy in weight_copies(ids[1], a3, b3, w3, par3, sem3) + weight_copies(ids[1], a4, b4, w4, par4, sem4):
        copy.start()
    layer_kernel(side, tiles, "full", None, 1, True, ids, near, even, odd, mt, a3, b3, kept, lines, w3, par3, sem3, *space)
    layer_kernel(side, tiles, "ring", 1, 0, True, ids, near, kept, lines, mt, a4, b4, out, w4, par4, sem4, *space)


def work_space(side, tiles, ch, depth_out):
    px = side * side
    halves = ch // LANES
    lines = 4 * depth_out if depth_out else 1
    line_rows = lines * side * (tiles - 2) if depth_out else 2 * side
    return [
        pltpu.VMEM((tiles, halves, px, LANES), F32),
        pltpu.VMEM((halves, px, LANES), F32),
        pltpu.VMEM((tiles, lines, side, ch), BF16),
        pltpu.VMEM((4, halves, side, LANES), F32),
        pltpu.VMEM((4, halves, 1, LANES), F32),
        pltpu.VMEM((2, side + 2, 3, side, ch), BF16),
        pltpu.VMEM((2 * px, 9 * ch), BF16),
        pltpu.VMEM((2 * px, ch), F32),
        pltpu.VMEM((line_rows, 9 * ch), BF16),
        pltpu.VMEM((line_rows, ch), F32),
    ]


def weight_space(ch):
    return [pltpu.VMEM((9 * ch, ch), BF16), pltpu.VMEM((EXTRA, ch), BF16), pltpu.SemaphoreType.DMA((3,))]


def limit(operands, scratch):
    sizes = [math.prod(item.shape) * jnp.dtype(item.dtype).itemsize for item in operands]
    sizes += [math.prod(item.shape) * jnp.dtype(item.dtype).itemsize for item in scratch if item.memory_space == pltpu.VMEM]
    return sum(sizes) + 6 * 2**20


def last_layers(side, tiles, ids, near, even, odd, mt, weights):
    ch = even.shape[-1]
    px = side * side
    kept = (2, px, ch)
    scratch = [pltpu.VMEM(kept, BF16), pltpu.VMEM((tiles - 2, 4, side, ch), BF16)]
    scratch += weight_space(ch) + weight_space(ch) + work_space(side, tiles, ch, 1)
    return pl.pallas_call(
        functools.partial(last_layers_kernel, side, tiles),
        out_shape=jax.ShapeDtypeStruct(kept, BF16),
        in_specs=[SMEM, SMEM, VMEM, VMEM, VMEM] + [HBM] * 4,
        out_specs=VMEM,
        scratch_shapes=scratch,
        compiler_params=pltpu.CompilerParams(vmem_limit_bytes=limit((even, odd, mt), scratch)),
        cost_estimate=pl.CostEstimate(flops=1, bytes_accessed=1, transcendentals=0),
    )(ids, near, even, odd, mt, *weights)


def layer(side, tiles, source, depth_in, depth_out, ids, near, data, weights):
    ch = weights[0].shape[-1]
    px = side * side
    halves = ch // LANES
    copied = source != "payload"
    if depth_out is None:
        shapes = [jax.ShapeDtypeStruct((tiles // 2, px, ch), BF16)]
        if not copied:
            shapes.append(jax.ShapeDtypeStruct((tiles, px, LANES), F32))
    else:
        shapes = [jax.ShapeDtypeStruct((2, px, ch), BF16)]
        if depth_out:
            shapes.append(jax.ShapeDtypeStruct((tiles - 2, 4 * depth_out, side, ch), BF16))
    scratch = (weight_space(ch) if copied else []) + work_space(side, tiles, ch, depth_out)
    return pl.pallas_call(
        functools.partial(layer_kernel, side, tiles, source, depth_in, depth_out, False),
        out_shape=shapes,
        in_specs=[SMEM, SMEM] + [VMEM] * len(data) + [HBM if copied else VMEM] * 2,
        out_specs=[VMEM] * len(shapes),
        scratch_shapes=scratch,
        compiler_params=pltpu.CompilerParams(vmem_limit_bytes=limit((*data, *weights, *shapes), scratch)),
        cost_estimate=pl.CostEstimate(flops=1, bytes_accessed=1, transcendentals=0),
    )(ids, near, *data, *weights)


def local(activations, weight, conv_bias, norm_gain, metric, neighbours):
    sections = lax.axis_size("section")
    tiles = lax.axis_size("tile")
    own = lax.axis_index("tile")
    core = own & 1
    group = (own >> 1) & 1
    side, ch = activations.shape[2], activations.shape[-1]
    px = side * side
    ids = jnp.stack([own, core, group]).astype(jnp.int32)

    flat = weight.reshape(-1, ch)
    mine, other, half = pack(ids, activations.reshape(2, px, ch), metric.reshape(9, px), flat, norm_gain, conv_bias)
    arrived = [fetch(half, "section", k) for k in range(1, sections)]

    going = neighbours[0, 0, 0] >= 0

    def fenced(step, *operands):
        shape = jax.eval_shape(step, *operands)
        blank = lambda *_: jax.tree.map(lambda leaf: jnp.zeros(leaf.shape, leaf.dtype), shape)
        return lax.cond(going, step, blank, *operands)

    even = [mine]
    for by in range(2, tiles, 2):
        even.append(swap(other if by & 2 else mine, "tile", by))
    even = jnp.stack(even)
    odd = swap(even, "tile", 1)

    def begin(even, odd):
        return layer(side, tiles, "payload", None, None, ids, neighbours, (even, odd), (flat, half[-EXTRA:]))

    states, spread_metric = fenced(begin, even, odd)
    for k in range(1, sections - 2):

        def proceed(states, spread_metric, a):
            weights = (a, swap(a, "tile", 1))
            data = (states, swap(states, "tile", 1), spread_metric)
            return layer(side, tiles, "full", None, None, ids, neighbours, data, weights)[0]

        states = fenced(proceed, states, spread_metric, arrived[k - 1])

    def finish(states, spread_metric, a, b):
        weights = (a, swap(a, "tile", 1), b, swap(b, "tile", 1))
        return last_layers(side, tiles, ids, neighbours, states, swap(states, "tile", 1), spread_metric, weights)

    done = fenced(finish, states, spread_metric, arrived[-2], arrived[-1])
    back = swap(done[1], "tile", 2)
    out = jnp.where(group == 0, jnp.stack([done[0], back]), jnp.stack([back, done[0]]))
    return out.reshape(activations.shape)


def solution(mesh):
    in_specs = (
        P("section", "tile", None, None, None),
        P("section", None, None, None),
        P("section", None),
        P("section", None),
        P("tile", None, None),
        P(),
    )
    out_specs = P("section", "tile", None, None, None)
    return jax.shard_map(local, mesh=mesh, in_specs=in_specs, out_specs=out_specs, check_vma=False)
```

```python
import functools
import math

import jax
import jax.numpy as jnp
from jax import lax
from jax.experimental import pallas as pl
from jax.experimental.pallas import tpu as pltpu
from jax.sharding import PartitionSpec as P

BF16 = jnp.bfloat16
F32 = jnp.float32
EXTRA = 16
LANES = 128


def swap(value, axis, by):
    peers = lax.axis_size(axis)
    return lax.ppermute(value, axis, [(i, i ^ by) for i in range(peers)])


def fetch(value, axis, by):
    peers = lax.axis_size(axis)
    return lax.ppermute(value, axis, [((i + by) % peers, i) for i in range(peers)])


def ring_lines(side, depth):
    lines = []
    for d in range(depth):
        lines += [("row", d), ("row", side - 1 - d), ("col", d), ("col", side - 1 - d)]
    return lines


def weight_copies(core, half_a, half_b, w, par, sem):
    rows = half_a.shape[0] - EXTRA
    at_a = pl.multiple_of(core * rows, LANES)
    at_b = pl.multiple_of((1 - core) * rows, LANES)
    return [
        pltpu.make_async_copy(half_a.at[pl.ds(0, rows)], w.at[pl.ds(at_a, rows)], sem.at[0]),
        pltpu.make_async_copy(half_b.at[pl.ds(0, rows)], w.at[pl.ds(at_b, rows)], sem.at[1]),
        pltpu.make_async_copy(half_a.at[pl.ds(rows, EXTRA)], par, sem.at[2]),
    ]


def layer_kernel(side, tiles, source, depth_in, depth_out, started, *refs):
    refs = list(refs)
    take = lambda n: [refs.pop(0) for _ in range(n)]
    px = side * side
    ids, near = take(2)
    if source == "payload":
        even, odd = take(2)
    elif source == "full":
        even, odd, mt = take(3)
    else:
        kept_in, lines_in, mt = take(3)
    copied = source != "payload"
    weights = take(2)
    outs = take(2 if depth_out is None and source == "payload" or depth_out else 1)
    if copied:
        w, par, sem = take(3)
    else:
        w, par = weights
    zf, vtmp, vlines, fr, cr, pads, x, acc, xo, acco = take(10)
    if source == "payload":
        mt = outs[1]
    ch = x.shape[1] // 9
    halves = ch // LANES
    own, core = ids[0], ids[1]
    lines_out = ring_lines(side, depth_out or 0)
    step = min(64, px)
    chunks = [slice(i, i + step) for i in range(0, px, step)]

    if copied:
        copies = weight_copies(core, *weights, w, par, sem)
        if not started:
            for copy in copies:
                copy.start()
        copies[2].wait()
    gain = par[0:1, :].astype(F32)
    bias = par[1:2, :].astype(F32)

    def normed(part):
        mean_sq = jnp.mean(part * part, axis=-1, keepdims=True)
        return (part * lax.rsqrt(mean_sq + 1e-05) * gain).astype(BF16).astype(F32)

    def by_lanes(value):
        return [value[:, h * LANES : (h + 1) * LANES] for h in range(halves)]

    def at_line(kind, at):
        return pl.ds(at * side, side) if kind == "row" else pl.ds(at, side, stride=side)

    def normed_tile(b, read):
        for part in chunks:
            v = read(part)
            for h, value in enumerate(by_lanes(normed(v))):
                zf[b, h, part] = value
            if depth_out:
                for h, value in enumerate(by_lanes(v)):
                    vtmp[h, part] = value
        for n, (kind, at) in enumerate(lines_out):
            for h in range(halves):
                vlines[b, n, :, h * LANES : (h + 1) * LANES] = vtmp[h, at_line(kind, at), :].astype(BF16)

    def other(i):
        return jnp.where(i == 0, 1, i + 2)

    if source == "payload":

        @pl.loop(0, tiles // 2)
        def _(j):
            for ref, b in ((even, 2 * j), (odd, 2 * j + 1)):
                normed_tile(b, lambda part: ref[j, part].astype(F32))
                mt[b, 0:px, 0:EXTRA] = jnp.transpose(ref[j, px : px + EXTRA, :].astype(F32))

    elif source == "full":

        @pl.loop(0, tiles // 2)
        def _(j):
            for ref, b in ((even, 2 * j), (odd, 2 * j + 1)):
                normed_tile(b, lambda part: ref[j, part].astype(F32))

    else:
        for place in range(2):
            for part in chunks:
                for h, value in enumerate(by_lanes(normed(kept_in[place, part].astype(F32)))):
                    zf[2 * place, h, part] = value
        lines = ring_lines(side, depth_in)

        @pl.loop(0, tiles - 2)
        def _(i):
            b = other(i)
            for first in range(0, len(lines), 4):
                z = normed(lines_in[i, first : first + 4].astype(F32).reshape(4 * side, ch))
                for n in range(4):
                    kind, at = lines[first + n]
                    for h, value in enumerate(by_lanes(z[n * side : (n + 1) * side])):
                        zf[b, h, at_line(kind, at), :] = value

    if copied:
        copies[0].wait()
        copies[1].wait()

    place_of = lax.broadcasted_iota(jnp.int32, (side, LANES), 0)
    eight = lax.broadcasted_iota(jnp.int32, (8, LANES), 0)
    first_place, last_place = place_of == 0, place_of == side - 1

    def frames(b):
        tile = own ^ b
        for s in range(4):
            src = own ^ near[0, tile, s]
            which = near[1, tile, s]
            flip = near[2, tile, s] == 1
            by_row = (which == 0) | (which == 2)
            at_row = pl.multiple_of(jnp.where(which == 0, 0, px - side), side)
            at_col = jnp.where(which == 1, side - 1, 0)
            for h in range(halves):
                line = jnp.where(by_row, zf[src, h, pl.ds(at_row, side), :], zf[src, h, pl.ds(at_col, side, stride=side), :])
                groups = [line[g : g + 8] for g in range(0, side, 8)]
                for n, group in enumerate(groups):
                    turned = pltpu.roll(groups[-1 - n], 4, 0)
                    for bit in (2, 1):
                        turned = jnp.where(eight & bit != 0, pltpu.roll(turned, bit, 0), pltpu.roll(turned, 8 - bit, 0))
                    fr[s, h, 8 * n : 8 * n + 8] = jnp.where(flip, turned, group)
        for k in range(4):
            src = own ^ near[0, tile, 4 + k]
            which = near[1, tile, 4 + k]
            at = jnp.where(which < 2, 0, px - side) + jnp.where((which == 1) | (which == 2), side - 1, 0)
            for h in range(halves):
                cr[k, h] = zf[src, h, pl.ds(at, 1), :]

    def spread(place, n, h, line, before, after):
        lanes = slice(h * LANES, (h + 1) * LANES)
        pads[place, n, 0, :, lanes] = jnp.where(first_place, before, pltpu.roll(line, 1, 0)).astype(BF16)
        pads[place, n, 1, :, lanes] = line.astype(BF16)
        pads[place, n, 2, :, lanes] = jnp.where(last_place, after, pltpu.roll(line, side - 1, 0)).astype(BF16)

    def spread_line(place, n, b, kind, at):
        low, high = (3, 1) if kind == "row" else (0, 2)
        for h in range(halves):
            if at < 0 or at >= side:
                edge = {("row", -1): (0, 0, 1), ("row", side): (2, 3, 2), ("col", -1): (3, 0, 3), ("col", side): (1, 1, 2)}
                s, k_before, k_after = edge[kind, at]
                spread(place, n, h, fr[s, h], cr[k_before, h], cr[k_after, h])
            else:
                line = zf[b, h, at_line(kind, at), :]
                spread(place, n, h, line, fr[low, h, at : at + 1], fr[high, h, at : at + 1])

    def build_tile(b, place):
        frames(b)
        for at in range(-1, side + 1):
            spread_line(place, at + 1, b, "row", at)
        metric = mt[b, 0:px]
        for q in range(9):
            a, c = q // 3, q % 3
            taps = jnp.broadcast_to(metric[:, q : q + 1], (px, LANES)).astype(BF16)
            for lane in range(0, ch, LANES):
                x[place * px : (place + 1) * px, q * ch + lane : q * ch + lane + LANES] = (
                    pads[place, a : a + side, c, :, lane : lane + LANES].reshape(px, LANES) * taps
                )

    def build_lines(b, i):
        frames(b)
        slots = {}
        for kind, at in lines_out:
            for near_at in (at - 1, at, at + 1):
                if (kind, near_at) not in slots:
                    slots[kind, near_at] = len(slots)
                    spread_line(0, slots[kind, near_at], b, kind, near_at)
        for n, (kind, at) in enumerate(lines_out):
            metric = mt[b, at_line(kind, at), :]
            row = pl.multiple_of((i * len(lines_out) + n) * side, side)
            for q in range(9):
                a, c = q // 3, q % 3
                slot, seen = (slots[kind, at + a - 1], c) if kind == "row" else (slots[kind, at + c - 1], a)
                taps = jnp.broadcast_to(metric[:, q : q + 1], (side, LANES)).astype(BF16)
                for lane in range(0, ch, LANES):
                    lanes = slice(lane, lane + LANES)
                    xo[pl.ds(row, side), q * ch + lane : q * ch + lane + LANES] = pads[0, slot, seen, :, lanes] * taps

    def updated(v, conv):
        u = conv + bias
        return (v.astype(F32) + u / (1.0 + jnp.exp(-u))).astype(BF16)

    if depth_out is None:

        @pl.loop(0, tiles // 4)
        def _(j):
            build_tile(4 * j, 0)
            build_tile(4 * j + 2, 1)
            acc[...] = jnp.dot(x[...], w[...], preferred_element_type=F32)
            for place in range(2):
                for part in chunks:
                    conv = acc[place * px + part.start : place * px + part.stop]
                    outs[0][2 * j + place, part] = updated(even[2 * j + place, part], conv)

    else:
        build_tile(0, 0)
        build_tile(2, 1)
        acc[...] = jnp.dot(x[...], w[...], preferred_element_type=F32)
        for place in range(2):
            for part in chunks:
                v = even[place, part] if source == "full" else kept_in[place, part]
                outs[0][place, part] = updated(v, acc[place * px + part.start : place * px + part.stop])
        if depth_out:

            @pl.loop(0, tiles - 2)
            def _(i):
                build_lines(other(i), i)

            acco[...] = jnp.dot(xo[...], w[...], preferred_element_type=F32)

            @pl.loop(0, tiles - 2)
            def _(i):
                count = len(lines_out)
                for first in range(0, count, 4):
                    v = vlines[other(i), first : first + 4] if source == "full" else lines_in[i, first : first + 4]
                    at = pl.multiple_of((i * count + first) * side, side)
                    new = updated(v.reshape(4 * side, ch), acco[pl.ds(at, 4 * side)])
                    outs[1][i, first : first + 4] = new.reshape(4, side, ch)


def pack_kernel(ids, batches, metric, flat, gain, bias, mine, other, half, sem):
    px, ch = batches.shape[1:]
    rows = half.shape[0] - EXTRA
    start = pl.multiple_of(ids[1] * rows, LANES)
    copies = [
        pltpu.make_async_copy(batches.at[ids[2]], mine.at[pl.ds(0, px)], sem.at[0]),
        pltpu.make_async_copy(batches.at[1 - ids[2]], other.at[pl.ds(0, px)], sem.at[1]),
        pltpu.make_async_copy(flat.at[pl.ds(start, rows)], half.at[pl.ds(0, rows)], sem.at[2]),
    ]
    for copy in copies:
        copy.start()
    spare = jnp.concatenate([metric[...], jnp.zeros((EXTRA - 9, px), BF16)], axis=0)
    mine[px : px + EXTRA, :] = spare
    other[px : px + EXTRA, :] = spare
    half[rows : rows + EXTRA, :] = jnp.concatenate([gain[...], bias[...], jnp.zeros((EXTRA - 2, ch), BF16)], axis=0)
    for copy in copies:
        copy.wait()


def pack(ids, batches, metric, flat, gain, bias):
    state = jax.ShapeDtypeStruct((batches.shape[1] + EXTRA, batches.shape[2]), BF16)
    half = jax.ShapeDtypeStruct((flat.shape[0] // 2 + EXTRA, flat.shape[1]), BF16)
    return pl.pallas_call(
        pack_kernel,
        out_shape=(state, state, half),
        in_specs=[SMEM, HBM, VMEM, HBM, VMEM, VMEM],
        out_specs=(VMEM, VMEM, VMEM),
        scratch_shapes=[pltpu.SemaphoreType.DMA((3,))],
        compiler_params=pltpu.CompilerParams(vmem_limit_bytes=60 * 2**20),
    )(ids, batches, metric, flat, gain, bias)


VMEM = pl.BlockSpec(memory_space=pltpu.VMEM)
SMEM = pl.BlockSpec(memory_space=pltpu.SMEM)
HBM = pl.BlockSpec(memory_space=pl.ANY)


def last_layers_kernel(side, tiles, *refs):
    ids, near, even, odd, mt, a3, b3, a4, b4, out, kept, lines = refs[:12]
    w3, par3, sem3, w4, par4, sem4 = refs[12:18]
    space = refs[18:]
    for copy in weight_copies(ids[1], a3, b3, w3, par3, sem3) + weight_copies(ids[1], a4, b4, w4, par4, sem4):
        copy.start()
    layer_kernel(side, tiles, "full", None, 1, True, ids, near, even, odd, mt, a3, b3, kept, lines, w3, par3, sem3, *space)
    layer_kernel(side, tiles, "ring", 1, 0, True, ids, near, kept, lines, mt, a4, b4, out, w4, par4, sem4, *space)


def work_space(side, tiles, ch, depth_out):
    px = side * side
    halves = ch // LANES
    lines = 4 * depth_out if depth_out else 1
    line_rows = lines * side * (tiles - 2) if depth_out else 2 * side
    return [
        pltpu.VMEM((tiles, halves, px + side, LANES), F32),
        pltpu.VMEM((halves, px + side, LANES), F32),
        pltpu.VMEM((tiles, lines, side, ch), BF16),
        pltpu.VMEM((4, halves, side, LANES), F32),
        pltpu.VMEM((4, halves, 1, LANES), F32),
        pltpu.VMEM((2, side + 2, 3, side, ch), BF16),
        pltpu.VMEM((2 * px, 9 * ch), BF16),
        pltpu.VMEM((2 * px, ch), F32),
        pltpu.VMEM((line_rows, 9 * ch), BF16),
        pltpu.VMEM((line_rows, ch), F32),
    ]


def weight_space(ch):
    return [pltpu.VMEM((9 * ch, ch), BF16), pltpu.VMEM((EXTRA, ch), BF16), pltpu.SemaphoreType.DMA((3,))]


def limit(operands, scratch):
    sizes = [math.prod(item.shape) * jnp.dtype(item.dtype).itemsize for item in operands]
    sizes += [math.prod(item.shape) * jnp.dtype(item.dtype).itemsize for item in scratch if item.memory_space == pltpu.VMEM]
    return sum(sizes) + 6 * 2**20


def last_layers(side, tiles, ids, near, even, odd, mt, weights):
    ch = even.shape[-1]
    px = side * side
    kept = (2, px, ch)
    scratch = [pltpu.VMEM(kept, BF16), pltpu.VMEM((tiles - 2, 4, side, ch), BF16)]
    scratch += weight_space(ch) + weight_space(ch) + work_space(side, tiles, ch, 1)
    return pl.pallas_call(
        functools.partial(last_layers_kernel, side, tiles),
        out_shape=jax.ShapeDtypeStruct(kept, BF16),
        in_specs=[SMEM, SMEM, VMEM, VMEM, VMEM] + [HBM] * 4,
        out_specs=VMEM,
        scratch_shapes=scratch,
        compiler_params=pltpu.CompilerParams(vmem_limit_bytes=limit((even, odd, mt), scratch)),
        cost_estimate=pl.CostEstimate(flops=1, bytes_accessed=1, transcendentals=0),
    )(ids, near, even, odd, mt, *weights)


def layer(side, tiles, source, depth_in, depth_out, ids, near, data, weights):
    ch = weights[0].shape[-1]
    px = side * side
    halves = ch // LANES
    copied = source != "payload"
    if depth_out is None:
        shapes = [jax.ShapeDtypeStruct((tiles // 2, px, ch), BF16)]
        if not copied:
            shapes.append(jax.ShapeDtypeStruct((tiles, px + side, LANES), F32))
    else:
        shapes = [jax.ShapeDtypeStruct((2, px, ch), BF16)]
        if depth_out:
            shapes.append(jax.ShapeDtypeStruct((tiles - 2, 4 * depth_out, side, ch), BF16))
    scratch = (weight_space(ch) if copied else []) + work_space(side, tiles, ch, depth_out)
    return pl.pallas_call(
        functools.partial(layer_kernel, side, tiles, source, depth_in, depth_out, False),
        out_shape=shapes,
        in_specs=[SMEM, SMEM] + [VMEM] * len(data) + [HBM if copied else VMEM] * 2,
        out_specs=[VMEM] * len(shapes),
        scratch_shapes=scratch,
        compiler_params=pltpu.CompilerParams(vmem_limit_bytes=limit((*data, *weights, *shapes), scratch)),
        cost_estimate=pl.CostEstimate(flops=1, bytes_accessed=1, transcendentals=0),
    )(ids, near, *data, *weights)


def local(activations, weight, conv_bias, norm_gain, metric, neighbours):
    sections = lax.axis_size("section")
    tiles = lax.axis_size("tile")
    own = lax.axis_index("tile")
    core = own & 1
    group = (own >> 1) & 1
    side, ch = activations.shape[2], activations.shape[-1]
    px = side * side
    ids = jnp.stack([own, core, group]).astype(jnp.int32)

    flat = weight.reshape(-1, ch)
    mine, other, half = pack(ids, activations.reshape(2, px, ch), metric.reshape(9, px), flat, norm_gain, conv_bias)
    arrived = [fetch(half, "section", k) for k in range(1, sections)]

    going = neighbours[0, 0, 0] >= 0

    def fenced(step, *operands):
        shape = jax.eval_shape(step, *operands)
        blank = lambda *_: jax.tree.map(lambda leaf: jnp.zeros(leaf.shape, leaf.dtype), shape)
        return lax.cond(going, step, blank, *operands)

    even = [mine]
    for by in range(2, tiles, 2):
        even.append(swap(other if by & 2 else mine, "tile", by))
    even = jnp.stack(even)
    odd = swap(even, "tile", 1)

    def begin(even, odd):
        return layer(side, tiles, "payload", None, None, ids, neighbours, (even, odd), (flat, half[-EXTRA:]))

    states, spread_metric = fenced(begin, even, odd)
    for k in range(1, sections - 2):

        def proceed(states, spread_metric, a):
            weights = (a, swap(a, "tile", 1))
            data = (states, swap(states, "tile", 1), spread_metric)
            return layer(side, tiles, "full", None, None, ids, neighbours, data, weights)[0]

        states = fenced(proceed, states, spread_metric, arrived[k - 1])

    def finish(states, spread_metric, a, b):
        weights = (a, swap(a, "tile", 1), b, swap(b, "tile", 1))
        return last_layers(side, tiles, ids, neighbours, states, swap(states, "tile", 1), spread_metric, weights)

    done = fenced(finish, states, spread_metric, arrived[-2], arrived[-1])
    back = swap(done[1], "tile", 2)
    out = jnp.where(group == 0, jnp.stack([done[0], back]), jnp.stack([back, done[0]]))
    return out.reshape(activations.shape)


def solution(mesh):
    in_specs = (
        P("section", "tile", None, None, None),
        P("section", None, None, None),
        P("section", None),
        P("section", None),
        P("tile", None, None),
        P(),
    )
    out_specs = P("section", "tile", None, None, None)
    return jax.shard_map(local, mesh=mesh, in_specs=in_specs, out_specs=out_specs, check_vma=False)
```
